1024 devices in a mesh: group: 32 (over y, x), slot: 32 (over z, core).
Axes of the slice: x: 4, y: 8, z: 16, core: 2. Of those that a mesh axis runs over, the one named last changes fastest.
Arguments:
- tokens: bfloat16 [131072, 2048], P(('group', 'slot')), may hold values from -6 to 6
- cotangent: bfloat16 [131072, 512], P(('group', 'slot')), may hold values from -0.59765625 to 0.59765625
- weight_halves: bfloat16 [1024, 1024, 512], P(('group', 'slot')), may hold values from -0.125 to 0.125
- momentum_halves: bfloat16 [1024, 1024, 512], P(('group', 'slot')), may hold values from -6 to 6
- old_map: int32 [32, 16], replicated, may hold values from 0 to 15, each once within a row
- new_map: int32 [32, 32], replicated, may hold values from 0 to 15, as said below
- row_ids: int32 [1024, 128], P(('group', 'slot')), may hold values from 0 to 127
Outputs:
- projected: bfloat16 [131072, 512], P(('group', 'slot'))
The draws below stay inside these ranges and needn't reach their ends.
Inputs may be any that keep to these rules, and one draw needn't show every extreme that they name: `old_map`: each row names each of the group's experts once. `new_map`: every expert is hosted by one to four new slots; among the experts of every owner group one is hosted by exactly four.
All inputs are finite; a program needn't handle non-finite values.
Results may differ from the reference program's by a relative error of at most 0.007.
Values may be sent and summed in bfloat16 or wider, within the bound.
A program may use at most 32 MiB of HBM per device.

```python
import math
import jax
import jax.numpy as jnp
from jax import lax

D = 2048
H = 512
R_OLD = 128
R_NEW = 128
ITERS = 2
EXP_GRP = 16
HOSTS = 1
BLK = 32
N_GROUP = 32
N_SLOT = 32


def draw_new_map(key, part):
    per_group = N_SLOT // 2
    pair_count = (per_group - 4) // 2

    def one_source(sub_key):
        first_key, second_key, third_key = jax.random.split(sub_key, 3)
        order = jax.random.permutation(first_key, per_group).astype(jnp.int32)
        lower = jax.random.randint(second_key, (pair_count,), 1, 4).astype(jnp.int32)
        counts = jnp.concatenate([jnp.array([4, 1, 2, 1], jnp.int32), jnp.stack([lower, 4 - lower], axis=1).reshape(-1)])
        listed = jnp.repeat(order, counts, total_repeat_length=N_SLOT)
        return jax.random.permutation(third_key, listed)
    lists = jax.vmap(one_source)(jax.random.split(jax.random.fold_in(key, 7), N_GROUP))
    arranged = jnp.transpose(lists.reshape(N_GROUP, N_GROUP, N_SLOT // N_GROUP), (1, 0, 2))
    return arranged.reshape(N_GROUP, N_SLOT).astype(jnp.int32)


def with_ends(values, rng, least, high):
    longest = values.shape.index(max(values.shape))
    spots = []
    for shift in (0, 1):
        where = [jax.random.randint(jax.random.fold_in(rng, axis), (), 0, length) for axis, length in enumerate(values.shape)]
        where[longest] = (where[longest] + shift) % values.shape[longest]
        spots.append(tuple(where))
    return values.at[spots[0]].set(least).at[spots[1]].set(high)


def levels(key, shape, pieces, least, top_value):
    def one(position, parts):
        draws = jax.random.uniform(jax.random.fold_in(jax.random.fold_in(key, 6), position), (parts,), jnp.float32, least / len(pieces), top_value / len(pieces))
        return jnp.repeat(jnp.exp(draws), shape[position] // parts).reshape((-1,) + (1,) * (len(shape) - position - 1))

    loudness = one(*pieces[0])
    for cut in pieces[1:]:
        loudness = loudness * one(*cut)
    return loudness


def scatter_about(key, extent, width, most, shards=(), kind=jnp.bfloat16):
    entries = width * jax.random.normal(key, extent, jnp.float32)
    if shards:
        entries = entries * levels(key, extent, shards, -0.22, 0.18)
    return jnp.clip(entries, -most, most).astype(kind)


def setup_inputs(seed: int = 0) -> dict:
    streams_of = jax.random.split(jax.random.key(seed), 8)
    tokens = scatter_about(streams_of[0], (N_GROUP * N_SLOT * R_OLD, D), 1.0, 6.0, ((0, 1024),))
    cotangent = scatter_about(streams_of[1], (N_GROUP * N_SLOT * R_OLD, H), 0.1, 0.59765625, ((0, 1024),))
    weight_halves = scatter_about(streams_of[2], (N_GROUP * N_SLOT, D // 2, H), D ** -0.5, 0.125, ((0, 1024),))
    momentum_halves = scatter_about(streams_of[3], (N_GROUP * N_SLOT, D // 2, H), 1.0, 6.0, ((0, 1024),))
    old_map = jax.vmap(lambda own: jax.random.permutation(own, EXP_GRP))(jax.random.split(streams_of[4], N_GROUP)).reshape((N_GROUP, EXP_GRP)).astype(jnp.int32)
    new_map = draw_new_map(jax.random.fold_in(streams_of[7], 71), 0)
    row_ids = with_ends(jax.random.randint(streams_of[6], (N_GROUP * N_SLOT, R_NEW), 0, R_OLD), jax.random.fold_in(streams_of[6], 1), 0, R_OLD - 1).astype(jnp.int32)
    return {"tokens": tokens, "cotangent": cotangent, "weight_halves": weight_halves, "momentum_halves": momentum_halves, "old_map": old_map, "new_map": new_map, "row_ids": row_ids}


coef_a = 3.4445
coef_b = -4.775
coef_c = 2.0315
momentum_rate = 0.95
step_scale = 0.01
gram_eps = 1e-06

def split_rows(full_matrix, which_half):
    blocks_view = full_matrix.reshape(N_SLOT, 2, BLK, H)
    return blocks_view[:, which_half].reshape(D // 2, H)

def join_rows(first_half, second_half):
    stacked = jnp.stack([first_half.reshape(N_SLOT, BLK, H), second_half.reshape(N_SLOT, BLK, H)], axis=1)
    return stacked.reshape(D, H)

def rounded(value):
    return lax.optimization_barrier(value.astype(jnp.bfloat16)).astype(jnp.float32)

def half_gram(half_rows):
    return rounded(jnp.dot(half_rows.T, half_rows, preferred_element_type=jnp.float32))

def full_gram(current):
    return half_gram(split_rows(current, 0)) + half_gram(split_rows(current, 1))

def update_expert(bundle):
    token_pair, cot_pair, weight_pair, moment_pair = bundle
    gradient = rounded(jnp.dot(token_pair[0].T, cot_pair[0], preferred_element_type=jnp.float32))
    gradient = gradient + rounded(jnp.dot(token_pair[1].T, cot_pair[1], preferred_element_type=jnp.float32))
    moment = join_rows(moment_pair[0], moment_pair[1]).astype(jnp.float32)
    current = (momentum_rate * moment + gradient).astype(jnp.bfloat16)
    gram_sum = full_gram(current)
    norm_sq = jnp.trace(gram_sum) + gram_eps
    for iteration in range(ITERS):
        if iteration == 0:
            scaled = gram_sum / norm_sq
            factor = 1.0 / jnp.sqrt(norm_sq)
        else:
            scaled = gram_sum
            factor = 1.0
        gram_bf = scaled.astype(jnp.bfloat16)
        square = jnp.dot(gram_bf, gram_bf, preferred_element_type=jnp.float32)
        polynomial = (coef_b * scaled + coef_c * square).astype(jnp.bfloat16)
        product = jnp.dot(current, polynomial, preferred_element_type=jnp.float32)
        current = (factor * (coef_a * current.astype(jnp.float32) + product)).astype(jnp.bfloat16)
        if iteration + 1 < ITERS:
            gram_sum = full_gram(current)
    weight = join_rows(weight_pair[0], weight_pair[1]).astype(jnp.float32)
    return (weight - step_scale * math.sqrt(D) * current.astype(jnp.float32)).astype(jnp.bfloat16)

def per_group(bundle):
    return lax.map(update_expert, bundle)

def reference(tokens, cotangent, weight_halves, momentum_halves, old_map, new_map, row_ids):
    token_rows = tokens.reshape(N_GROUP, EXP_GRP, 2, R_OLD, D)
    cot_rows = cotangent.reshape(N_GROUP, EXP_GRP, 2, R_OLD, H)
    weight_rows = weight_halves.reshape(N_GROUP, EXP_GRP, 2, D // 2, H)
    moment_rows = momentum_halves.reshape(N_GROUP, EXP_GRP, 2, D // 2, H)
    updated = lax.map(per_group, (token_rows, cot_rows, weight_rows, moment_rows))
    expert_iota = jnp.arange(EXP_GRP, dtype=jnp.int32)
    where_held = jnp.argmax((old_map[:, None, :] == expert_iota[None, :, None]).astype(jnp.int32), axis=2).astype(jnp.int32)
    slot_iota = jnp.arange(N_SLOT, dtype=jnp.int32)
    source = jnp.broadcast_to((slot_iota // HOSTS)[None, :], (N_GROUP, N_SLOT)).astype(jnp.int32)
    holder = where_held[source, new_map].astype(jnp.int32)
    flat_tokens = tokens.reshape(N_GROUP * N_SLOT, R_OLD, D)

    def project(bundle):
        own_tokens, own_ids, own_source, own_holder = bundle
        weight = updated[own_source, own_holder]
        chosen = jnp.take(own_tokens, own_ids, axis=0)
        return jnp.dot(chosen, weight, preferred_element_type=jnp.float32).astype(jnp.bfloat16)
    projected = lax.map(project, (flat_tokens, row_ids, source.reshape(-1), holder.reshape(-1)))
    return projected.reshape(N_GROUP * N_SLOT * R_NEW, H)
```

```python
import functools
import math

import jax
import jax.numpy as jnp
from jax import lax
from jax.experimental import pallas as pl
from jax.experimental.pallas import tpu as pltpu
from jax.sharding import PartitionSpec as P

ITERS = 2
CAP = 4
BLK = 32
SUB = 2
MESH = pl.DeviceIdType.MESH
BF16, F32 = jnp.bfloat16, jnp.float32
VMEM = pltpu.VMEM
DMA = pltpu.SemaphoreType.DMA

coef_a = 3.4445
coef_b = -4.775
coef_c = 2.0315
momentum_rate = 0.95
step_scale = 0.01
gram_eps = 1e-06
ROWS = (((0,), (0,)), ((), ()))


def dot(a, b):
    return jnp.dot(a, b, preferred_element_type=F32)


def dot_rows(a, b):
    return lax.dot_general(a, b, ROWS, preferred_element_type=F32)


def loop(count, body):
    lax.fori_loop(0, count, lambda i, c: (body(i), c)[1], 0)


def kernel(
    groups, slots,
    table, tokens, cot, rows, weight_hbm, moment_hbm,
    out,
    weight, moment, halves, picked, got_parts, sent, landed, result, spread, back, answer, final,
    own_part, send_part, peer_part, x, gram, gram_peer, total, poly, full,
    load_sem, p_send, p_recv, f_send, f_recv, a_send, a_recv, r_send, r_recv, b_send, b_recv,
    g_send, g_recv, m_send, m_recv, w_send, w_recv,
):
    g, s = lax.axis_index("group"), lax.axis_index("slot")
    h = lax.rem(s, 2)
    mate = (g, s + 1 - 2 * h)
    n_rows, width = tokens.shape
    hidden = cot.shape[1]
    half = width // 2
    diagonal = g == s

    barrier = pltpu.get_barrier_semaphore()

    def hello(device):
        pl.semaphore_signal(barrier, inc=1, device_id=device, device_id_type=MESH)

    loop(groups - 1, lambda i: hello((lax.rem(g + 1 + i, groups), s)))
    loop(slots - 1, lambda i: hello((g, lax.rem(s + 1 + i, slots))))

    def hello_sender(i):
        c = lax.rem(s + i, groups)

        @pl.when(jnp.logical_not(jnp.logical_and(diagonal, c == g)))
        def _():
            hello((c, g))

    loop(groups, hello_sender)

    load_w = pltpu.make_async_copy(weight_hbm.at[0], weight, load_sem.at[0])
    load_m = pltpu.make_async_copy(moment_hbm.at[0], moment, load_sem.at[1])
    load_w.start()
    load_m.start()

    wide = 8 * BLK
    col = lax.broadcasted_iota(jnp.int32, (wide, wide), 1)
    row = lax.broadcasted_iota(jnp.int32, (wide, wide), 0)
    inner = col % (wide // 2)
    origin = (inner // BLK) * (2 * BLK) + (col // (wide // 2)) * BLK + inner % BLK
    order = (row == origin).astype(F32).astype(BF16)
    pick = (lax.broadcasted_iota(jnp.int32, (n_rows, n_rows), 0) == rows[...]).astype(F32).astype(BF16)
    for b in range(width // wide):
        sorted_cols = dot(tokens[:, b * wide : (b + 1) * wide], order).astype(BF16)
        chosen = dot_rows(pick, sorted_cols).astype(BF16)
        for k in range(2):
            where = slice(b * wide // 2, (b + 1) * wide // 2)
            piece = slice(k * wide // 2, (k + 1) * wide // 2)
            halves[k, :, where] = sorted_cols[:, piece]
            picked[:, k * half + where.start : k * half + where.stop] = chosen[:, piece]

    tall = n_rows // SUB
    high = tall // 16
    across = groups // high
    cw = width // across

    def piece_of(q, c):
        return picked.at[
            pl.ds(pl.multiple_of(q * tall + (c // across) * 16, 16), 16),
            pl.ds(pl.multiple_of(lax.rem(c, across) * cw, cw), cw),
        ]

    @pl.when(diagonal)
    def _():
        pl.semaphore_wait(barrier, groups - 1 + slots - 1 + slots - 1)

    @pl.when(jnp.logical_not(diagonal))
    def _():
        pl.semaphore_wait(barrier, groups - 1 + slots - 1 + slots)

    for q in range(SUB):

        def send_piece(i, q=q):
            c = lax.rem(g + 1 + i, groups)
            pltpu.make_async_remote_copy(
                piece_of(q, c), got_parts[q].at[g], p_send, p_recv.at[q], device_id=(c, s), device_id_type=MESH
            ).start()

        loop(groups - 1, send_piece)
        pltpu.make_async_copy(piece_of(q, g), got_parts[q].at[g], p_recv.at[q]).start()

    parts = 2
    tile = half // parts
    grads = []
    for part in range(parts):
        where = pl.ds(part * tile, tile)
        send_part[where, :] = dot_rows(halves[1 - h, :, part * tile : (part + 1) * tile], cot[...]).astype(BF16)
        copy = pltpu.make_async_remote_copy(
            send_part.at[where], peer_part.at[where], g_send.at[part], g_recv.at[part],
            device_id=mate, device_id_type=MESH,
        )
        copy.start()
        grads.append(copy)
    for part in range(parts):
        own_part[pl.ds(part * tile, tile), :] = dot_rows(
            halves[h, :, part * tile : (part + 1) * tile], cot[...]
        ).astype(BF16)

    def forward(k, q):
        def select(t):
            sent[k, q, t] = got_parts[q][table[(t // 2) * CAP + 2 * k + lax.rem(t, 2)]]

        loop(slots, select)
        place = landed.at[
            k,
            pl.ds(pl.multiple_of(q * tall + (g // across) * 16, 16), 16),
            pl.ds(pl.multiple_of(lax.rem(g, across) * cw, cw), cw),
        ]

        def send(i):
            t = lax.rem(s + 1 + i, slots)
            itself = jnp.logical_and(diagonal, t == s)

            @pl.when(jnp.logical_not(itself))
            def _():
                pltpu.make_async_remote_copy(
                    sent.at[k, q, t], place, f_send, f_recv.at[k], device_id=(s, t), device_id_type=MESH
                ).start()

            @pl.when(itself)
            def _():
                pltpu.make_async_copy(sent.at[k, q, t], place, f_recv.at[k]).start()

        loop(slots, send)

    def wait_pieces(q):
        pltpu.make_async_copy(got_parts[q], got_parts[q], p_recv.at[q]).wait()

    for q in range(SUB):
        wait_pieces(q)
        forward(0, q)
    for q in range(SUB):
        forward(1, q)

    chunk = 256

    def share_gram(t):
        total[...] = jnp.zeros_like(total)

        def add(i):
            block = x[pl.ds(pl.multiple_of(i * chunk, chunk), chunk), :]
            total[...] += dot_rows(block, block)

        loop(half // chunk, add)
        gram[t] = total[...].astype(BF16)
        copy = pltpu.make_async_remote_copy(
            gram.at[t], gram_peer.at[t], m_send.at[t], m_recv.at[t], device_id=mate, device_id_type=MESH
        )
        copy.start()
        return copy

    load_m.wait()
    for copy in grads:
        copy.wait_recv()

    def first(i):
        where = pl.ds(pl.multiple_of(i * chunk, chunk), chunk)
        grad = own_part[where, :].astype(F32) + peer_part[where, :].astype(F32)
        x[where, :] = (momentum_rate * moment[where, :].astype(F32) + grad).astype(BF16)

    loop(half // chunk, first)
    grams = []
    factor = None
    for t in range(ITERS):
        copy = share_gram(t)
        copy.wait_recv()
        grams.append(copy)
        both = gram[t].astype(F32) + gram_peer[t].astype(F32)
        if t == 0:
            on_diagonal = lax.broadcasted_iota(jnp.int32, both.shape, 0) == lax.broadcasted_iota(
                jnp.int32, both.shape, 1
            )
            norm_sq = jnp.sum(jnp.where(on_diagonal, both, 0.0), axis=(0, 1), keepdims=True) + gram_eps
            both = both / norm_sq
            factor = 1.0 / jnp.sqrt(norm_sq)
        total[...] = both
        gram_bf = both.astype(BF16)
        poly[...] = (coef_b * total[...] + coef_c * dot(gram_bf, gram_bf)).astype(BF16)
        if t + 1 == ITERS:
            load_w.wait()

        def step(i, t=t, factor=factor):
            where = pl.ds(pl.multiple_of(i * chunk, chunk), chunk)
            block = x[where, :]
            new = coef_a * block.astype(F32) + dot(block, poly[...])
            if t == 0:
                new = factor * new
            new = new.astype(BF16)
            if t + 1 < ITERS:
                x[where, :] = new
            else:
                full[h, where, :] = (
                    weight[where, :].astype(F32) - step_scale * math.sqrt(width) * new.astype(F32)
                ).astype(BF16)

        loop(half // chunk, step)
    whole = pltpu.make_async_remote_copy(
        full.at[h], full.at[h], w_send, w_recv, device_id=mate, device_id_type=MESH
    )
    whole.start()
    whole.wait_recv()

    out_high = n_rows // 16
    out_across = groups // out_high
    ow = hidden // out_across

    def tile_of(ref, c):
        return ref.at[
            pl.ds(pl.multiple_of((c // out_across) * 16, 16), 16),
            pl.ds(pl.multiple_of(lax.rem(c, out_across) * ow, ow), ow),
        ]

    for k in range(2):
        pltpu.make_async_copy(landed.at[k], landed.at[k], f_recv.at[k]).wait()
        product = dot(landed[k, :, :half], full[0]) + dot(landed[k, :, half:], full[1])
        result[k] = product.astype(BF16)

        def spread_out(i, k=k):
            c = lax.rem(g + 1 + i, groups)
            pltpu.make_async_remote_copy(
                tile_of(result.at[k], c), spread.at[k, g], a_send, a_recv.at[k, g],
                device_id=(c, s), device_id_type=MESH,
            ).start()

        loop(groups - 1, spread_out)
        pltpu.make_async_copy(tile_of(result.at[k], g), spread.at[k, g], a_recv.at[k, g]).start()

        def pass_on(i, k=k):
            o = lax.rem(g + lax.rem(i, 2) * groups + (1 - 2 * lax.rem(i, 2)) * ((i + 1) // 2), groups)
            pltpu.make_async_copy(spread.at[k, o], spread.at[k, o], a_recv.at[k, o]).wait()

            @pl.when(o != s)
            def _():
                pltpu.make_async_remote_copy(
                    spread.at[k, o], back.at[k * slots + s], r_send, r_recv.at[k],
                    device_id=(g, o), device_id_type=MESH,
                ).start()

            @pl.when(o == s)
            def _():
                pltpu.make_async_copy(spread.at[k, o], back.at[k * slots + s], r_recv.at[k]).start()

        loop(groups, pass_on)

    for k in range(2):
        these = back.at[pl.ds(k * slots, slots)]
        pltpu.make_async_copy(these, these, r_recv.at[k]).wait()

    def answer_one(c):
        answer[c] = back[table[slots * 2 + c]]

    loop(groups, answer_one)

    def give(i):
        c = lax.rem(g + 1 + i, groups)
        pltpu.make_async_remote_copy(
            answer.at[c], tile_of(final, g), b_send, b_recv, device_id=(c, s), device_id_type=MESH
        ).start()

    loop(groups - 1, give)
    pltpu.make_async_copy(answer.at[g], tile_of(final, g), b_recv).start()

    def left(ref, sem):
        pltpu.make_async_copy(ref, ref, sem).wait()

    for copy in grads + grams + [whole]:
        copy.wait_send()
    for q in range(SUB):
        left(got_parts[q].at[pl.ds(0, groups - 1)], p_send)
    for k in range(2):
        left(spread.at[k, pl.ds(0, groups - 1)], a_send)
        left(back.at[pl.ds(0, slots - 1)], r_send)
        for q in range(SUB):
            left(sent.at[k, q, pl.ds(0, slots - 1)], f_send)

            @pl.when(jnp.logical_not(diagonal))
            def _():
                left(sent.at[k, q, 0], f_send)

    left(answer.at[pl.ds(0, groups - 1)], b_send)
    pltpu.make_async_copy(final, final, b_recv).wait()
    out[...] = final[...]


def on_device(tokens, cotangent, weight_halves, momentum_halves, old_map, new_map, row_ids):
    slots, groups = lax.axis_size("slot"), lax.axis_size("group")
    n_rows, width = tokens.shape
    hidden = cotangent.shape[1]
    half = width // 2
    experts = slots // 2

    owner = lax.axis_index("slot")
    held = lax.dynamic_index_in_dim(old_map, owner, 0, keepdims=False)
    asked = lax.dynamic_index_in_dim(new_map, owner, 1, keepdims=False)
    one = jnp.arange(groups, dtype=jnp.int32)
    hit = (held[None, :] == asked[:, None]).astype(jnp.int32)
    holder = jnp.sum(hit * jnp.arange(experts, dtype=jnp.int32)[None, :], axis=1)
    earlier = (asked[None, :] == asked[:, None]) & (one[None, :] < one[:, None])
    rank = jnp.sum(earlier.astype(jnp.int32), axis=1)
    place = holder * CAP + rank
    mine = place[None, :] == jnp.arange(experts * CAP, dtype=jnp.int32)[:, None]
    source = jnp.sum(mine.astype(jnp.int32) * one[None, :], axis=1)
    origin = (rank // 2) * slots + holder * 2 + rank % 2
    table = jnp.concatenate([source, origin])

    tall = n_rows // SUB
    cw = width // (groups // (tall // 16))
    ow = hidden // (groups // (n_rows // 16))
    vm = pl.BlockSpec(memory_space=VMEM)
    hbm = pl.BlockSpec(memory_space=pl.ANY)
    return pl.pallas_call(
        functools.partial(kernel, groups, slots),
        out_shape=jax.ShapeDtypeStruct((n_rows, hidden), BF16),
        in_specs=[pl.BlockSpec(memory_space=pltpu.SMEM), vm, vm, vm, hbm, hbm],
        out_specs=vm,
        scratch_shapes=[
            VMEM((half, hidden), BF16),
            VMEM((half, hidden), BF16),
            VMEM((2, n_rows, half), BF16),
            VMEM((n_rows, width), BF16),
            [VMEM((groups, 16, cw), BF16)] * SUB,
            VMEM((2, SUB, slots, 16, cw), BF16),
            VMEM((2, n_rows, width), BF16),
            VMEM((2, n_rows, hidden), BF16),
            VMEM((2, groups, 16, ow), BF16),
            VMEM((2 * slots, 16, ow), BF16),
            VMEM((groups, 16, ow), BF16),
            VMEM((n_rows, hidden), BF16),
            VMEM((half, hidden), BF16),
            VMEM((half, hidden), BF16),
            VMEM((half, hidden), BF16),
            VMEM((half, hidden), BF16),
            VMEM((ITERS, hidden, hidden), BF16),
            VMEM((ITERS, hidden, hidden), BF16),
            VMEM((hidden, hidden), F32),
            VMEM((hidden, hidden), BF16),
            VMEM((2, half, hidden), BF16),
            DMA((2,)),
            DMA,
            DMA((SUB,)),
            DMA,
            DMA((2,)),
            DMA,
            DMA((2, groups)),
            DMA,
            DMA((2,)),
            DMA,
            DMA,
            DMA((2,)),
            DMA((2,)),
            DMA((ITERS,)),
            DMA((ITERS,)),
            DMA,
            DMA,
        ],
        compiler_params=pltpu.CompilerParams(
            collective_id=0, has_side_effects=True, vmem_limit_bytes=48 << 20
        ),
        name="muon_route",
    )(table, tokens, cotangent, row_ids, weight_halves, momentum_halves)


def solution(mesh):
    placed = (
        P(("group", "slot"), None),
        P(("group", "slot"), None),
        P(("group", "slot"), None, None),
        P(("group", "slot"), None, None),
        P(),
        P(),
        P(("group", "slot"), None),
    )
    return jax.shard_map(
        on_device, mesh=mesh, in_specs=placed, out_specs=P(("group", "slot"), None), check_vma=False
    )
```

```python
import functools
import math

import jax
import jax.numpy as jnp
from jax import lax
from jax.experimental import pallas as pl
from jax.experimental.pallas import tpu as pltpu
from jax.sharding import PartitionSpec as P

ITERS = 2
CAP = 4
BLK = 32
SUB = 4
MESH = pl.DeviceIdType.MESH
BF16, F32 = jnp.bfloat16, jnp.float32
VMEM = pltpu.VMEM
DMA = pltpu.SemaphoreType.DMA

coef_a = 3.4445
coef_b = -4.775
coef_c = 2.0315
momentum_rate = 0.95
step_scale = 0.01
gram_eps = 1e-06
ROWS = (((0,), (0,)), ((), ()))


def dot(a, b):
    return jnp.dot(a, b, preferred_element_type=F32)


def dot_rows(a, b):
    return lax.dot_general(a, b, ROWS, preferred_element_type=F32)


def loop(count, body):
    lax.fori_loop(0, count, lambda i, c: (body(i), c)[1], 0)


def kernel(
    groups, slots,
    old_map, new_map, rows, tokens_hbm, cot_hbm, weight_hbm, moment_hbm,
    out,
    tokens, cot, weight, moment, halves, table_rows, table, got_parts, sent, landed, result, spread, back, answer, final,
    own_part, send_part, peer_part, x, gram, gram_peer, total, poly, full,
    load_sem, p_send, p_recv, f_send, f_recv, a_send, a_recv, r_send, r_recv, b_send, b_recv,
    g_send, g_recv, m_send, m_recv, w_send, w_recv,
):
    g, s = lax.axis_index("group"), lax.axis_index("slot")
    h = lax.rem(s, 2)
    mate = (g, s + 1 - 2 * h)
    n_rows, width = tokens.shape
    hidden = cot.shape[1]
    half = width // 2
    diagonal = g == s

    loads = [
        pltpu.make_async_copy(source, target, load_sem.at[n])
        for n, (source, target) in enumerate(
            (
                (tokens_hbm, tokens),
                (cot_hbm, cot),
                (moment_hbm.at[0], moment),
                (weight_hbm.at[0], weight),
            )
        )
    ]
    for load in loads:
        load.start()

    barrier = pltpu.get_barrier_semaphore()

    def hello(device):
        pl.semaphore_signal(barrier, inc=1, device_id=device, device_id_type=MESH)

    loop(groups - 1, lambda i: hello((lax.rem(g + 1 + i, groups), s)))
    loop(slots - 1, lambda i: hello((g, lax.rem(s + 1 + i, slots))))

    def hello_sender(i):
        c = lax.rem(s + i, groups)

        @pl.when(jnp.logical_not(jnp.logical_and(diagonal, c == g)))
        def _():
            hello((c, g))

    loop(groups, hello_sender)

    tall = n_rows // SUB
    high = tall // 16
    across = groups // high
    cw = width // across

    def piece_of(q, c):
        return tokens.at[
            pl.ds(pl.multiple_of(q * tall + (c // across) * 16, 16), 16),
            pl.ds(pl.multiple_of(lax.rem(c, across) * cw, cw), cw),
        ]

    @pl.when(diagonal)
    def _():
        pl.semaphore_wait(barrier, groups - 1 + slots - 1 + slots - 1)

    @pl.when(jnp.logical_not(diagonal))
    def _():
        pl.semaphore_wait(barrier, groups - 1 + slots - 1 + slots)

    loads[0].wait()
    for q in range(SUB):

        def send_piece(i, q=q):
            c = lax.rem(g + 1 + i, groups)
            pltpu.make_async_remote_copy(
                piece_of(q, c), got_parts[q].at[g], p_send, p_recv.at[q], device_id=(c, s), device_id_type=MESH
            ).start()

        loop(groups - 1, send_piece)
        pltpu.make_async_copy(piece_of(q, g), got_parts[q].at[g], p_recv.at[q]).start()

    experts = slots // 2

    def iota(shape, axis):
        return lax.broadcasted_iota(jnp.int32, shape, axis)

    def total_of(mask, value, axis):
        return jnp.sum(jnp.where(mask, value, 0), axis=axis, keepdims=True)

    square = (groups, groups)
    asked = total_of(iota((groups, slots), 1) == s, new_map[...], 1)
    asked_row = total_of(iota(square, 0) == iota(square, 1), asked, 0)
    held = total_of(iota((experts, groups), 1) == s, old_map[...], 1)
    held = total_of(iota((experts, experts), 0) == iota((experts, experts), 1), held, 0)
    holder = total_of(asked == held, iota((groups, experts), 1), 1)
    earlier = jnp.logical_and(asked == asked_row, iota(square, 1) < iota(square, 0))
    rank = total_of(earlier, jnp.ones(square, jnp.int32), 1)
    rank_half = (rank >= 2).astype(jnp.int32)
    source = total_of(holder * CAP + rank == iota((groups, experts * CAP), 1), iota((groups, experts * CAP), 0), 0)
    table_rows[...] = jnp.zeros_like(table_rows)
    table_rows[0:1, 0 : experts * CAP] = jnp.minimum(source, groups - 1)
    origin = jnp.minimum(rank_half * slots + holder * 2 + rank - 2 * rank_half, 2 * slots - 1)
    table_rows[1:2, 0:groups] = total_of(iota(square, 0) == iota(square, 1), origin, 0)
    to_scalars = pltpu.make_async_copy(table_rows, table, load_sem.at[4])
    to_scalars.start()

    wide = 8 * BLK
    col = iota((wide, wide), 1)
    inner = col % (wide // 2)
    came_from = (inner // BLK) * (2 * BLK) + (col // (wide // 2)) * BLK + inner % BLK
    order = (iota((wide, wide), 0) == came_from).astype(F32).astype(BF16)
    for b in range(width // wide):
        sorted_cols = dot(tokens[:, b * wide : (b + 1) * wide], order).astype(BF16)
        for k in range(2):
            halves[k, :, b * wide // 2 : (b + 1) * wide // 2] = sorted_cols[
                :, k * wide // 2 : (k + 1) * wide // 2
            ]
    loads[1].wait()

    parts = 2
    tile = half // parts
    grads = []
    for part in range(parts):
        where = pl.ds(part * tile, tile)
        send_part[where, :] = dot_rows(halves[1 - h, :, part * tile : (part + 1) * tile], cot[...]).astype(BF16)
        copy = pltpu.make_async_remote_copy(
            send_part.at[where], peer_part.at[where], g_send.at[part], g_recv.at[part],
            device_id=mate, device_id_type=MESH,
        )
        copy.start()
        grads.append(copy)
    for part in range(parts):
        own_part[pl.ds(part * tile, tile), :] = dot_rows(
            halves[h, :, part * tile : (part + 1) * tile], cot[...]
        ).astype(BF16)

    def forward(rank_of, q):
        k, core = rank_of // 2, rank_of % 2

        def select(p):
            sent[k, q, 2 * p + core] = got_parts[q][table[0, p * CAP + rank_of]]

        loop(experts, select)
        place = landed.at[
            k,
            pl.ds(pl.multiple_of(q * tall + (g // across) * 16, 16), 16),
            pl.ds(pl.multiple_of(lax.rem(g, across) * cw, cw), cw),
        ]

        def send(i):
            t = 2 * lax.rem(s // 2 + 1 + i, experts) + core
            itself = jnp.logical_and(diagonal, t == s)

            @pl.when(jnp.logical_not(itself))
            def _():
                pltpu.make_async_remote_copy(
                    sent.at[k, q, t], place, f_send, f_recv.at[k], device_id=(s, t), device_id_type=MESH
                ).start()

            @pl.when(itself)
            def _():
                pltpu.make_async_copy(sent.at[k, q, t], place, f_recv.at[k]).start()

        loop(experts, send)

    def wait_pieces(q):
        pltpu.make_async_copy(got_parts[q], got_parts[q], p_recv.at[q]).wait()

    to_scalars.wait()
    for q in range(SUB):
        wait_pieces(q)
        forward(0, q)
    for rank_of in range(1, CAP):
        for q in range(SUB):
            forward(rank_of, q)

    chunk = 256

    def share_gram(t):
        total[...] = jnp.zeros_like(total)

        def add(i):
            block = x[pl.ds(pl.multiple_of(i * chunk, chunk), chunk), :]
            total[...] += dot_rows(block, block)

        loop(half // chunk, add)
        gram[t] = total[...].astype(BF16)
        copy = pltpu.make_async_remote_copy(
            gram.at[t], gram_peer.at[t], m_send.at[t], m_recv.at[t], device_id=mate, device_id_type=MESH
        )
        copy.start()
        return copy

    loads[2].wait()
    for copy in grads:
        copy.wait_recv()

    def first(i):
        where = pl.ds(pl.multiple_of(i * chunk, chunk), chunk)
        grad = own_part[where, :].astype(F32) + peer_part[where, :].astype(F32)
        x[where, :] = (momentum_rate * moment[where, :].astype(F32) + grad).astype(BF16)

    loop(half // chunk, first)
    grams = []
    factor = None
    for t in range(ITERS):
        copy = share_gram(t)
        copy.wait_recv()
        grams.append(copy)
        both = gram[t].astype(F32) + gram_peer[t].astype(F32)
        if t == 0:
            on_diagonal = lax.broadcasted_iota(jnp.int32, both.shape, 0) == lax.broadcasted_iota(
                jnp.int32, both.shape, 1
            )
            norm_sq = jnp.sum(jnp.where(on_diagonal, both, 0.0), axis=(0, 1), keepdims=True) + gram_eps
            both = both / norm_sq
            factor = 1.0 / jnp.sqrt(norm_sq)
        total[...] = both
        gram_bf = both.astype(BF16)
        poly[...] = (coef_b * total[...] + coef_c * dot(gram_bf, gram_bf)).astype(BF16)
        if t + 1 == ITERS:
            loads[3].wait()

        def step(i, t=t, factor=factor):
            where = pl.ds(pl.multiple_of(i * chunk, chunk), chunk)
            block = x[where, :]
            new = coef_a * block.astype(F32) + dot(block, poly[...])
            if t == 0:
                new = factor * new
            new = new.astype(BF16)
            if t + 1 < ITERS:
                x[where, :] = new
            else:
                renewed = weight[where, :].astype(F32) - step_scale * math.sqrt(width) * new.astype(F32)
                full[pl.ds(i * (chunk // BLK), chunk // BLK), h] = renewed.astype(BF16).reshape(
                    chunk // BLK, BLK, hidden
                )

        loop(half // chunk, step)
    whole = pltpu.make_async_remote_copy(
        full.at[:, h], full.at[:, h], w_send, w_recv, device_id=mate, device_id_type=MESH
    )
    whole.start()
    whole.wait_recv()

    out_high = n_rows // 16
    out_across = groups // out_high
    ow = hidden // out_across

    def tile_of(ref, c):
        return ref.at[
            pl.ds(pl.multiple_of((c // out_across) * 16, 16), 16),
            pl.ds(pl.multiple_of(lax.rem(c, out_across) * ow, ow), ow),
        ]

    for k in range(2):
        pltpu.make_async_copy(landed.at[k], landed.at[k], f_recv.at[k]).wait()
        result[k] = dot(landed[k], full[...].reshape(width, hidden)).astype(BF16)

        def spread_out(i, k=k):
            c = lax.rem(g + 1 + i, groups)
            pltpu.make_async_remote_copy(
                tile_of(result.at[k], c), spread.at[k, g], a_send, a_recv.at[k, g],
                device_id=(c, s), device_id_type=MESH,
            ).start()

        loop(groups - 1, spread_out)
        pltpu.make_async_copy(tile_of(result.at[k], g), spread.at[k, g], a_recv.at[k, g]).start()

        def pass_on(i, k=k):
            o = lax.rem(g + lax.rem(i, 2) * groups + (1 - 2 * lax.rem(i, 2)) * ((i + 1) // 2), groups)
            pltpu.make_async_copy(spread.at[k, o], spread.at[k, o], a_recv.at[k, o]).wait()

            @pl.when(o != s)
            def _():
                pltpu.make_async_remote_copy(
                    spread.at[k, o], back.at[k * slots + s], r_send, r_recv.at[k],
                    device_id=(g, o), device_id_type=MESH,
                ).start()

            @pl.when(o == s)
            def _():
                pltpu.make_async_copy(spread.at[k, o], back.at[k * slots + s], r_recv.at[k]).start()

        loop(groups, pass_on)

    for k in range(2):
        these = back.at[pl.ds(k * slots, slots)]
        pltpu.make_async_copy(these, these, r_recv.at[k]).wait()

    def answer_one(c):
        answer[c] = back[table[1, c]]

    loop(groups, answer_one)

    def give(i):
        c = lax.rem(g + 1 + i, groups)
        pltpu.make_async_remote_copy(
            answer.at[c], tile_of(final, g), b_send, b_recv, device_id=(c, s), device_id_type=MESH
        ).start()

    loop(groups - 1, give)
    pltpu.make_async_copy(answer.at[g], tile_of(final, g), b_recv).start()

    def left(ref, sem):
        pltpu.make_async_copy(ref, ref, sem).wait()

    for copy in grads + grams + [whole]:
        copy.wait_send()
    for q in range(SUB):
        left(got_parts[q].at[pl.ds(0, groups - 1)], p_send)
    for k in range(2):
        left(spread.at[k, pl.ds(0, groups - 1)], a_send)
        left(back.at[pl.ds(0, slots - 1)], r_send)
        for q in range(SUB):
            left(sent.at[k, q, pl.ds(0, slots - 1)], f_send)

            @pl.when(jnp.logical_not(diagonal))
            def _():
                left(sent.at[k, q, 0], f_send)

    left(answer.at[pl.ds(0, groups - 1)], b_send)
    pltpu.make_async_copy(final, final, b_recv).wait()
    pick = (iota((n_rows, n_rows), 0) == rows[...]).astype(F32).astype(BF16)
    out[...] = dot_rows(pick, final[...]).astype(BF16)


def on_device(tokens, cotangent, weight_halves, momentum_halves, old_map, new_map, row_ids):
    slots, groups = lax.axis_size("slot"), lax.axis_size("group")
    n_rows, width = tokens.shape
    hidden = cotangent.shape[1]
    half = width // 2
    tall = n_rows // SUB
    cw = width // (groups // (tall // 16))
    ow = hidden // (groups // (n_rows // 16))
    vm = pl.BlockSpec(memory_space=VMEM)
    hbm = pl.BlockSpec(memory_space=pl.ANY)
    return pl.pallas_call(
        functools.partial(kernel, groups, slots),
        out_shape=jax.ShapeDtypeStruct((n_rows, hidden), BF16),
        in_specs=[vm, vm, vm, hbm, hbm, hbm, hbm],
        out_specs=vm,
        scratch_shapes=[
            VMEM((n_rows, width), BF16),
            VMEM((n_rows, hidden), BF16),
            VMEM((half, hidden), BF16),
            VMEM((half, hidden), BF16),
            VMEM((2, n_rows, half), BF16),
            VMEM((8, 128), jnp.int32),
            pltpu.SMEM((8, 128), jnp.int32),
            [VMEM((groups, 16, cw), BF16)] * SUB,
            VMEM((2, SUB, slots, 16, cw), BF16),
            VMEM((2, n_rows, width), BF16),
            VMEM((2, n_rows, hidden), BF16),
            VMEM((2, groups, 16, ow), BF16),
            VMEM((2 * slots, 16, ow), BF16),
            VMEM((groups, 16, ow), BF16),
            VMEM((n_rows, hidden), BF16),
            VMEM((half, hidden), BF16),
            VMEM((half, hidden), BF16),
            VMEM((half, hidden), BF16),
            VMEM((half, hidden), BF16),
            VMEM((ITERS, hidden, hidden), BF16),
            VMEM((ITERS, hidden, hidden), BF16),
            VMEM((hidden, hidden), F32),
            VMEM((hidden, hidden), BF16),
            VMEM((half // BLK, 2, BLK, hidden), BF16),
            DMA((5,)),
            DMA,
            DMA((SUB,)),
            DMA,
            DMA((2,)),
            DMA,
            DMA((2, groups)),
            DMA,
            DMA((2,)),
            DMA,
            DMA,
            DMA((2,)),
            DMA((2,)),
            DMA((ITERS,)),
            DMA((ITERS,)),
            DMA,
            DMA,
        ],
        compiler_params=pltpu.CompilerParams(
            collective_id=0, has_side_effects=True, vmem_limit_bytes=60 << 20
        ),
        name="muon_route",
    )(old_map.T, new_map, row_ids, tokens, cotangent, weight_halves, momentum_halves)


def solution(mesh):
    placed = (
        P(("group", "slot"), None),
        P(("group", "slot"), None),
        P(("group", "slot"), None, None),
        P(("group", "slot"), None, None),
        P(),
        P(),
        P(("group", "slot"), None),
    )
    return jax.shard_map(
        on_device, mesh=mesh, in_specs=placed, out_specs=P(("group", "slot"), None), check_vma=False
    )
```

```python
import functools
import math

import jax
import jax.numpy as jnp
from jax import lax
from jax.experimental import pallas as pl
from jax.experimental.pallas import tpu as pltpu
from jax.sharding import PartitionSpec as P

ITERS = 2
CAP = 4
BLK = 32
SUB = 4
MESH = pl.DeviceIdType.MESH
BF16, F32 = jnp.bfloat16, jnp.float32
VMEM = pltpu.VMEM
DMA = pltpu.SemaphoreType.DMA

coef_a = 3.4445
coef_b = -4.775
coef_c = 2.0315
momentum_rate = 0.95
step_scale = 0.01
gram_eps = 1e-06
ROWS = (((0,), (0,)), ((), ()))


def dot(a, b):
    return jnp.dot(a, b, preferred_element_type=F32)


def dot_rows(a, b):
    return lax.dot_general(a, b, ROWS, preferred_element_type=F32)


def loop(count, body):
    lax.fori_loop(0, count, lambda i, c: (body(i), c)[1], 0)


def kernel(
    groups, slots,
    old_map, new_map, rows, tokens_hbm, cot_hbm, weight_hbm, moment_hbm,
    out,
    tokens, cot, weight, moment, halves, table_rows, table, got_parts, sent, landed, result, spread, back, answer, final,
    own_part, send_part, peer_part, x, gram, gram_peer, total, poly, full,
    load_sem, p_send, p_recv, f_send, f_recv, a_send, a_recv, r_send, r_recv, b_send, b_recv,
    g_send, g_recv, m_send, m_recv, w_send, w_recv,
):
    g, s = lax.axis_index("group"), lax.axis_index("slot")
    h = lax.rem(s, 2)
    mate = (g, s + 1 - 2 * h)
    n_rows, width = tokens.shape
    hidden = cot.shape[1]
    half = width // 2
    diagonal = g == s

    loads = [
        pltpu.make_async_copy(source, target, load_sem.at[n])
        for n, (source, target) in enumerate(
            (
                (tokens_hbm, tokens),
                (cot_hbm, cot),
                (moment_hbm.at[0], moment),
                (weight_hbm.at[0], weight),
            )
        )
    ]
    for load in loads:
        load.start()

    barrier = pltpu.get_barrier_semaphore()

    def hello(device):
        pl.semaphore_signal(barrier, inc=1, device_id=device, device_id_type=MESH)

    loop(groups - 1, lambda i: hello((lax.rem(g + 1 + i, groups), s)))
    loop(slots - 1, lambda i: hello((g, lax.rem(s + 1 + i, slots))))

    def hello_sender(i):
        c = lax.rem(s + i, groups)

        @pl.when(jnp.logical_not(jnp.logical_and(diagonal, c == g)))
        def _():
            hello((c, g))

    loop(groups, hello_sender)

    tall = n_rows // SUB
    high = tall // 16
    across = groups // high
    cw = width // across

    def piece_of(q, c):
        return tokens.at[
            pl.ds(pl.multiple_of(q * tall + (c // across) * 16, 16), 16),
            pl.ds(pl.multiple_of(lax.rem(c, across) * cw, cw), cw),
        ]

    @pl.when(diagonal)
    def _():
        pl.semaphore_wait(barrier, groups - 1 + slots - 1 + slots - 1)

    @pl.when(jnp.logical_not(diagonal))
    def _():
        pl.semaphore_wait(barrier, groups - 1 + slots - 1 + slots)

    loads[0].wait()
    for q in range(SUB):

        def send_piece(i, q=q):
            c = lax.rem(g + 1 + i, groups)
            pltpu.make_async_remote_copy(
                piece_of(q, c), got_parts[q].at[g], p_send, p_recv.at[q], device_id=(c, s), device_id_type=MESH
            ).start()

        loop(groups - 1, send_piece)
        pltpu.make_async_copy(piece_of(q, g), got_parts[q].at[g], p_recv.at[q]).start()

    experts = slots // 2

    def iota(shape, axis):
        return lax.broadcasted_iota(jnp.int32, shape, axis)

    def total_of(mask, value, axis):
        return jnp.sum(jnp.where(mask, value, 0), axis=axis, keepdims=True)

    square = (groups, groups)
    asked = total_of(iota((groups, slots), 1) == s, new_map[...], 1)
    asked_row = total_of(iota(square, 0) == iota(square, 1), asked, 0)
    held = total_of(iota((experts, groups), 1) == s, old_map[...], 1)
    held = total_of(iota((experts, experts), 0) == iota((experts, experts), 1), held, 0)
    holder = total_of(asked == held, iota((groups, experts), 1), 1)
    earlier = jnp.logical_and(asked == asked_row, iota(square, 1) < iota(square, 0))
    rank = total_of(earlier, jnp.ones(square, jnp.int32), 1)
    rank_half = (rank >= 2).astype(jnp.int32)
    source = total_of(holder * CAP + rank == iota((groups, experts * CAP), 1), iota((groups, experts * CAP), 0), 0)
    table_rows[...] = jnp.zeros_like(table_rows)
    table_rows[0:1, 0 : experts * CAP] = jnp.minimum(source, groups - 1)
    origin = jnp.minimum(rank_half * slots + holder * 2 + rank - 2 * rank_half, 2 * slots - 1)
    table_rows[1:2, 0:groups] = total_of(iota(square, 0) == iota(square, 1), origin, 0)
    to_scalars = pltpu.make_async_copy(table_rows, table, load_sem.at[4])
    to_scalars.start()

    def forward(rank_of, q):
        k, core = rank_of // 2, rank_of % 2

        def select(p):
            sent[k, q, 2 * p + core] = got_parts[q][table[0, p * CAP + rank_of]]

        loop(experts, select)
        place = landed.at[
            k,
            pl.ds(pl.multiple_of(q * tall + (g // across) * 16, 16), 16),
            pl.ds(pl.multiple_of(lax.rem(g, across) * cw, cw), cw),
        ]

        def send(i):
            t = 2 * lax.rem(s // 2 + 1 + i, experts) + core
            itself = jnp.logical_and(diagonal, t == s)

            @pl.when(jnp.logical_not(itself))
            def _():
                pltpu.make_async_remote_copy(
                    sent.at[k, q, t], place, f_send, f_recv.at[k], device_id=(s, t), device_id_type=MESH
                ).start()

            @pl.when(itself)
            def _():
                pltpu.make_async_copy(sent.at[k, q, t], place, f_recv.at[k]).start()

        loop(experts, send)

    def wait_pieces(q):
        pltpu.make_async_copy(got_parts[q], got_parts[q], p_recv.at[q]).wait()

    to_scalars.wait()
    for q in range(SUB):
        wait_pieces(q)
        forward(0, q)
    for rank_of in range(1, CAP):
        for q in range(SUB):
            forward(rank_of, q)

    wide = 8 * BLK
    col = iota((wide, wide), 1)
    inner = col % (wide // 2)
    came_from = (inner // BLK) * (2 * BLK) + (col // (wide // 2)) * BLK + inner % BLK
    order = (iota((wide, wide), 0) == came_from).astype(F32).astype(BF16)
    for b in range(width // wide):
        sorted_cols = dot(tokens[:, b * wide : (b + 1) * wide], order).astype(BF16)
        for k in range(2):
            halves[k, :, b * wide // 2 : (b + 1) * wide // 2] = sorted_cols[
                :, k * wide // 2 : (k + 1) * wide // 2
            ]
    loads[1].wait()

    parts = 2
    tile = half // parts
    grads = []
    for part in range(parts):
        where = pl.ds(part * tile, tile)
        send_part[where, :] = dot_rows(halves[1 - h, :, part * tile : (part + 1) * tile], cot[...]).astype(BF16)
        copy = pltpu.make_async_remote_copy(
            send_part.at[where], peer_part.at[where], g_send.at[part], g_recv.at[part],
            device_id=mate, device_id_type=MESH,
        )
        copy.start()
        grads.append(copy)
    for part in range(parts):
        own_part[pl.ds(part * tile, tile), :] = dot_rows(
            halves[h, :, part * tile : (part + 1) * tile], cot[...]
        ).astype(BF16)

    chunk = 256

    def share_gram(t):
        total[...] = jnp.zeros_like(total)

        def add(i):
            block = x[pl.ds(pl.multiple_of(i * chunk, chunk), chunk), :]
            total[...] += dot_rows(block, block)

        loop(half // chunk, add)
        gram[t] = total[...].astype(BF16)
        copy = pltpu.make_async_remote_copy(
            gram.at[t], gram_peer.at[t], m_send.at[t], m_recv.at[t], device_id=mate, device_id_type=MESH
        )
        copy.start()
        return copy

    loads[2].wait()
    for copy in grads:
        copy.wait_recv()

    def first(i):
        where = pl.ds(pl.multiple_of(i * chunk, chunk), chunk)
        grad = own_part[where, :].astype(F32) + peer_part[where, :].astype(F32)
        x[where, :] = (momentum_rate * moment[where, :].astype(F32) + grad).astype(BF16)

    loop(half // chunk, first)
    grams = []
    factor = None
    for t in range(ITERS):
        copy = share_gram(t)
        copy.wait_recv()
        grams.append(copy)
        both = gram[t].astype(F32) + gram_peer[t].astype(F32)
        if t == 0:
            on_diagonal = lax.broadcasted_iota(jnp.int32, both.shape, 0) == lax.broadcasted_iota(
                jnp.int32, both.shape, 1
            )
            norm_sq = jnp.sum(jnp.where(on_diagonal, both, 0.0), axis=(0, 1), keepdims=True) + gram_eps
            both = both / norm_sq
            factor = 1.0 / jnp.sqrt(norm_sq)
        total[...] = both
        gram_bf = both.astype(BF16)
        poly[...] = (coef_b * total[...] + coef_c * dot(gram_bf, gram_bf)).astype(BF16)
        if t + 1 == ITERS:
            loads[3].wait()

        def step(i, t=t, factor=factor):
            where = pl.ds(pl.multiple_of(i * chunk, chunk), chunk)
            block = x[where, :]
            new = coef_a * block.astype(F32) + dot(block, poly[...])
            if t == 0:
                new = factor * new
            new = new.astype(BF16)
            if t + 1 < ITERS:
                x[where, :] = new
            else:
                renewed = weight[where, :].astype(F32) - step_scale * math.sqrt(width) * new.astype(F32)
                full[pl.ds(i * (chunk // BLK), chunk // BLK), h] = renewed.astype(BF16).reshape(
                    chunk // BLK, BLK, hidden
                )

        loop(half // chunk, step)
    whole = pltpu.make_async_remote_copy(
        full.at[:, h], full.at[:, h], w_send, w_recv, device_id=mate, device_id_type=MESH
    )
    whole.start()
    whole.wait_recv()

    out_high = n_rows // 16
    out_across = groups // out_high
    ow = hidden // out_across

    def tile_of(ref, c):
        return ref.at[
            pl.ds(pl.multiple_of((c // out_across) * 16, 16), 16),
            pl.ds(pl.multiple_of(lax.rem(c, out_across) * ow, ow), ow),
        ]

    for k in range(2):
        pltpu.make_async_copy(landed.at[k], landed.at[k], f_recv.at[k]).wait()
        result[k] = dot(landed[k], full[...].reshape(width, hidden)).astype(BF16)

        def spread_out(i, k=k):
            c = lax.rem(g + 1 + i, groups)
            pltpu.make_async_remote_copy(
                tile_of(result.at[k], c), spread.at[k, g], a_send, a_recv.at[k, g],
                device_id=(c, s), device_id_type=MESH,
            ).start()

        loop(groups - 1, spread_out)
        pltpu.make_async_copy(tile_of(result.at[k], g), spread.at[k, g], a_recv.at[k, g]).start()

        def pass_on(i, k=k):
            o = lax.rem(g + lax.rem(i, 2) * groups + (1 - 2 * lax.rem(i, 2)) * ((i + 1) // 2), groups)
            pltpu.make_async_copy(spread.at[k, o], spread.at[k, o], a_recv.at[k, o]).wait()

            @pl.when(o != s)
            def _():
                pltpu.make_async_remote_copy(
                    spread.at[k, o], back.at[k * slots + s], r_send, r_recv.at[k],
                    device_id=(g, o), device_id_type=MESH,
                ).start()

            @pl.when(o == s)
            def _():
                pltpu.make_async_copy(spread.at[k, o], back.at[k * slots + s], r_recv.at[k]).start()

        loop(groups, pass_on)

    for k in range(2):
        these = back.at[pl.ds(k * slots, slots)]
        pltpu.make_async_copy(these, these, r_recv.at[k]).wait()

    def answer_one(c):
        answer[c] = back[table[1, c]]

    loop(groups, answer_one)

    def give(i):
        c = lax.rem(g + 1 + i, groups)
        pltpu.make_async_remote_copy(
            answer.at[c], tile_of(final, g), b_send, b_recv, device_id=(c, s), device_id_type=MESH
        ).start()

    loop(groups - 1, give)
    pltpu.make_async_copy(answer.at[g], tile_of(final, g), b_recv).start()

    def left(ref, sem):
        pltpu.make_async_copy(ref, ref, sem).wait()

    for copy in grads + grams + [whole]:
        copy.wait_send()
    for q in range(SUB):
        left(got_parts[q].at[pl.ds(0, groups - 1)], p_send)
    for k in range(2):
        left(spread.at[k, pl.ds(0, groups - 1)], a_send)
        left(back.at[pl.ds(0, slots - 1)], r_send)
        for q in range(SUB):
            left(sent.at[k, q, pl.ds(0, slots - 1)], f_send)

            @pl.when(jnp.logical_not(diagonal))
            def _():
                left(sent.at[k, q, 0], f_send)

    left(answer.at[pl.ds(0, groups - 1)], b_send)
    pltpu.make_async_copy(final, final, b_recv).wait()
    pick = (iota((n_rows, n_rows), 0) == rows[...]).astype(F32).astype(BF16)
    out[...] = dot_rows(pick, final[...]).astype(BF16)


def on_device(tokens, cotangent, weight_halves, momentum_halves, old_map, new_map, row_ids):
    slots, groups = lax.axis_size("slot"), lax.axis_size("group")
    n_rows, width = tokens.shape
    hidden = cotangent.shape[1]
    half = width // 2
    tall = n_rows // SUB
    cw = width // (groups // (tall // 16))
    ow = hidden // (groups // (n_rows // 16))
    vm = pl.BlockSpec(memory_space=VMEM)
    hbm = pl.BlockSpec(memory_space=pl.ANY)
    return pl.pallas_call(
        functools.partial(kernel, groups, slots),
        out_shape=jax.ShapeDtypeStruct((n_rows, hidden), BF16),
        in_specs=[vm, vm, vm, hbm, hbm, hbm, hbm],
        out_specs=vm,
        scratch_shapes=[
            VMEM((n_rows, width), BF16),
            VMEM((n_rows, hidden), BF16),
            VMEM((half, hidden), BF16),
            VMEM((half, hidden), BF16),
            VMEM((2, n_rows, half), BF16),
            VMEM((8, 128), jnp.int32),
            pltpu.SMEM((8, 128), jnp.int32),
            [VMEM((groups, 16, cw), BF16)] * SUB,
            VMEM((2, SUB, slots, 16, cw), BF16),
            VMEM((2, n_rows, width), BF16),
            VMEM((2, n_rows, hidden), BF16),
            VMEM((2, groups, 16, ow), BF16),
            VMEM((2 * slots, 16, ow), BF16),
            VMEM((groups, 16, ow), BF16),
            VMEM((n_rows, hidden), BF16),
            VMEM((half, hidden), BF16),
            VMEM((half, hidden), BF16),
            VMEM((half, hidden), BF16),
            VMEM((half, hidden), BF16),
            VMEM((ITERS, hidden, hidden), BF16),
            VMEM((ITERS, hidden, hidden), BF16),
            VMEM((hidden, hidden), F32),
            VMEM((hidden, hidden), BF16),
            VMEM((half // BLK, 2, BLK, hidden), BF16),
            DMA((5,)),
            DMA,
            DMA((SUB,)),
            DMA,
            DMA((2,)),
            DMA,
            DMA((2, groups)),
            DMA,
            DMA((2,)),
            DMA,
            DMA,
            DMA((2,)),
            DMA((2,)),
            DMA((ITERS,)),
            DMA((ITERS,)),
            DMA,
            DMA,
        ],
        compiler_params=pltpu.CompilerParams(
            collective_id=0, has_side_effects=True, vmem_limit_bytes=60 << 20
        ),
        name="muon_route",
    )(old_map.T, new_map, row_ids, tokens, cotangent, weight_halves, momentum_halves)


def solution(mesh):
    placed = (
        P(("group", "slot"), None),
        P(("group", "slot"), None),
        P(("group", "slot"), None, None),
        P(("group", "slot"), None, None),
        P(),
        P(),
        P(("group", "slot"), None),
    )
    return jax.shard_map(
        on_device, mesh=mesh, in_specs=placed, out_specs=P(("group", "slot"), None), check_vma=False
    )
```
